32 devices in a mesh: groups: 2 (over x), ex: 4 (over y, core), layer: 4 (over z).
Axes of the slice: x: 2, y: 2, z: 4, core: 2. Of those that a mesh axis runs over, the one named last changes fastest.
Arguments:
- query_grads: bfloat16 [4, 256, 4096], P('layer', 'ex')
- train_grads: bfloat16 [4, 4096, 4096], P('layer', ('groups', 'ex')), parts along dimension 1
- panels: bfloat16 [4, 4096, 4096], P('layer', 'ex'), as said below
- counts: int32 [8], P(('groups', 'ex')), parts along dimension 0, may hold values from 128 to 512, as said below
Outputs:
- scores: float32 [256, 4096], P('layer', ('groups', 'ex')), parts along dimension 1
The draws below stay inside these ranges and needn't reach their ends.
There are 2 independent parts, one for each index of `groups`. The reference program is written for one: setup_inputs(seed, part) draws one part's arguments, and reference() takes and returns one part's arrays. A program takes and returns all parts, laid end to end along the dimension named above; an argument that names none is the same for every part. Nothing has to cross between parts.
Inputs may be any that keep to these rules, and one draw needn't show every extreme that they name: `counts`: each device's count lies between 128 and 512; in every draw some device has exactly 512 live examples. `panels`: each panel is symmetric.
All inputs are finite; a program needn't handle non-finite values.
Results may differ from the reference program's by a relative error of at most 0.0029.
Values may be sent and summed in bfloat16 or wider, within the bound.
A program may use at most 64 MiB of HBM per device.

```python
import math
import jax
import jax.numpy as jnp

P_SIZE = 4096
TRDEV = 512
LAYERS = 4
TRAIN = 2048
NQ = 256
N_EX = 4


def scaled_grads(key, rows):
    first, second, third = jax.random.split(key, 3)
    noise = jax.random.normal(first, (LAYERS, rows, P_SIZE), jnp.float32)
    row_scale = jnp.exp(jax.random.uniform(second, (LAYERS, rows, 1), jnp.float32, math.log(0.3), math.log(3.0)))
    col_scale = jnp.exp(jax.random.uniform(third, (LAYERS, 1, P_SIZE), jnp.float32, math.log(0.3), math.log(3.0)))
    return (noise * row_scale * col_scale).astype(jnp.bfloat16)


def draw_query_grads(key, part):
    key = jax.random.fold_in(key, 11)
    return scaled_grads(key, NQ)


def draw_train_grads(key, part):
    key = jax.random.fold_in(key, 13)
    return scaled_grads(key, TRAIN)


def draw_panels(key, part):
    key = jax.random.fold_in(key, 17)
    first, second = jax.random.split(key)
    spread = jax.random.normal(first, (LAYERS, P_SIZE, P_SIZE), jnp.float32) * (0.5 / math.sqrt(P_SIZE))
    mirrored = spread + jnp.swapaxes(spread, 1, 2)
    diagonal = jnp.exp(jax.random.uniform(second, (LAYERS, P_SIZE, 1), jnp.float32, math.log(0.5), math.log(2.0)))
    identity = jnp.eye(P_SIZE, dtype=jnp.float32)[None, :, :]
    return (mirrored + diagonal * identity).astype(jnp.bfloat16)


def draw_counts(key, part):
    key = jax.random.fold_in(key, 19)
    first, second = jax.random.split(key)
    values = jax.random.randint(first, (N_EX,), TRDEV // 4, TRDEV + 1, jnp.int32)
    fullest = jax.random.randint(second, (), 0, N_EX, jnp.int32)
    slots = jnp.arange(N_EX, dtype=jnp.int32)
    return jnp.where(slots == fullest, TRDEV, values).astype(jnp.int32)


def setup_inputs(seed: int = 0, part: int = 0) -> dict:
    arg_keys = jax.random.split(jax.random.key(seed), 5)
    own_keys = jax.random.split(jax.random.fold_in(arg_keys[4], part), 5)
    return {
        "query_grads": draw_query_grads(jax.random.fold_in(arg_keys[4], 71), part),
        "train_grads": draw_train_grads(jax.random.fold_in(jax.random.fold_in(arg_keys[4], part), 71), part),
        "panels": draw_panels(jax.random.fold_in(arg_keys[4], 71), part),
        "counts": draw_counts(jax.random.fold_in(jax.random.fold_in(arg_keys[4], part), 71), part),
    }


def reference(query_grads, train_grads, panels, counts):
    raw = jnp.zeros((NQ, TRAIN), jnp.float32)
    for layer_index in range(LAYERS):
        conditioned = jnp.dot(query_grads[layer_index], panels[layer_index], preferred_element_type=jnp.float32).astype(jnp.bfloat16)
        raw = raw + jnp.dot(conditioned, train_grads[layer_index].T, preferred_element_type=jnp.float32)
    positions = jnp.arange(TRAIN, dtype=jnp.int32)
    owners = positions // TRDEV
    alive = (positions % TRDEV < counts[owners]).astype(jnp.float32)
    return raw * alive[None, :] / math.sqrt(LAYERS * P_SIZE)
```

```python
import functools
import math

import jax
import jax.numpy as jnp
from jax import lax
from jax.experimental import pallas as pl
from jax.experimental.pallas import tpu as pltpu
from jax.sharding import PartitionSpec as P

MESH = pl.DeviceIdType.MESH
NT = (((1,), (1,)), ((), ()))
CHUNK = 256


def per_device(query_grads, train_grads, panels, counts):
    train_rows = train_grads[0]
    panel_rows = panels[0]
    column_part = lax.dot_general(
        lax.all_gather(query_grads, "ex", axis=1, tiled=True)[0],
        panel_rows,
        NT,
        preferred_element_type=jnp.float32,
    ).astype(jnp.bfloat16)
    partial_scores = lax.dot_general(
        lax.all_gather(column_part, "ex", axis=1, tiled=True),
        train_rows,
        NT,
        preferred_element_type=jnp.float32,
    )
    alive_mask = (lax.iota(jnp.int32, train_rows.shape[0]) < counts[0]).astype(jnp.float32)
    partial_scores = partial_scores * alive_mask[None, :]
    summed = lax.psum_scatter(partial_scores, "layer", scatter_dimension=0, tiled=True)
    factor = 1.0 / math.sqrt(lax.axis_size("layer") * panel_rows.shape[1])
    return summed * factor


def kernel(layers, q_ref, t_ref, p_ref, o_ref, qbuf, pbuf, tbuf, cbuf, sbuf, sends, lands, loc, psem, send, recv):
    g, e, l = lax.axis_index("groups"), lax.axis_index("ex"), lax.axis_index("layer")
    y, c = e // 2, e % 2
    o = 1 - g
    yo, co = 1 - y, 1 - c
    far = 2 * yo + c
    mate, ypart, xpart = (g, 2 * y + co, l), (g, far, l), (o, e, l)
    half = q_ref.shape[1]
    pair = 2 * half
    depth = p_ref.shape[0]

    def remote(k, src, dst, dev):
        return pltpu.make_async_remote_copy(
            src_ref=src, dst_ref=dst, send_sem=send.at[k], recv_sem=recv.at[k], device_id=dev, device_id_type=MESH
        )

    def qat(yy, hh, cc):
        return qbuf.at[yy, pl.ds(pl.multiple_of(hh * pair + cc * half, half), half), :]

    def rows(hh):
        return pl.ds(pl.multiple_of(hh * pair, pair), pair)

    def cat(ee, yy, hh):
        return cbuf.at[ee, yy, rows(hh), :]

    own = [pltpu.make_async_copy(q_ref.at[h], qat(y, h, c), loc.at[h]) for h in range(2)]
    pcopy = [
        pltpu.make_async_copy(p_ref.at[pl.ds(j * CHUNK, CHUNK), :], pbuf.at[pl.ds(j * CHUNK, CHUNK), :], psem.at[j])
        for j in range(depth // CHUNK)
    ]
    tcopy = pltpu.make_async_copy(t_ref, tbuf, loc.at[2])
    for d in own + pcopy + [tcopy]:
        d.start()

    barrier = pltpu.get_barrier_semaphore()
    zpeers = [(g, e, lax.rem(l + d, layers)) for d in range(1, layers)]
    for dev in [mate, ypart, xpart] + zpeers:
        pl.semaphore_signal(barrier, inc=1, device_id=dev, device_id_type=MESH)
    pl.semaphore_wait(barrier, 2 + layers)

    cp = {}

    def start(k, src, dst, dev):
        cp[k] = remote(k, src, dst, dev)
        cp[k].start()

    start(0, q_ref.at[g], qat(y, g, c), ypart)
    for h in range(2):
        start(1 + h, q_ref.at[h], qat(y, h, c), mate)

    def condition(get_rows, put, first):
        @pl.loop(0, depth // CHUNK)
        def _(j):
            cols = pl.ds(pl.multiple_of(j * CHUNK, CHUNK), CHUNK)
            if first:
                pltpu.make_async_copy(p_ref.at[cols, :], pbuf.at[cols, :], psem.at[j]).wait()
            put(cols, lax.dot_general(get_rows(), pbuf[cols, :], NT, preferred_element_type=jnp.float32))

    for d in own:
        d.wait()
    cp[1].wait_recv()
    cp[2].wait_recv()

    def put_near(cols, v):
        cbuf[e, y, :, cols] = v.astype(jnp.bfloat16)

    condition(lambda: qbuf[y], put_near, True)
    start(8, cat(e, y, g), cat(e, y, g), ypart)
    for h in range(2):
        start(6 + h, cat(e, y, h), cat(e, y, h), mate)

    cp[0].wait_recv()
    start(3, qat(yo, g, c), qat(yo, g, c), mate)
    start(4, qat(yo, g, c), qat(yo, g, c), xpart)
    cp[3].wait_recv()

    def put_far(h):
        def put(cols, v):
            cbuf[e, yo, rows(h), cols] = v.astype(jnp.bfloat16)

        return put

    condition(lambda: qbuf[yo, rows(g), :], put_far(g), False)
    start(9, cat(e, yo, g), cat(e, yo, g), ypart)
    start(10, cat(e, yo, g), cat(e, yo, g), mate)

    cp[8].wait_recv()
    start(12, cat(far, yo, g), cat(far, yo, g), xpart)
    start(13, cat(far, yo, g), cat(far, yo, g), mate)

    cp[4].wait_recv()
    start(5, qat(yo, o, c), qat(yo, o, c), mate)
    cp[5].wait_recv()
    condition(lambda: qbuf[yo, rows(o), :], put_far(o), False)
    start(11, cat(e, yo, o), cat(e, yo, o), mate)

    cp[9].wait_recv()
    start(14, cat(far, y, g), cat(far, y, g), xpart)
    start(15, cat(far, y, g), cat(far, y, g), mate)

    def score(h, base):
        @pl.loop(0, t_ref.shape[0] // CHUNK)
        def _(j):
            slots = pl.ds(pl.multiple_of(j * CHUNK, CHUNK), CHUNK)
            acc = jnp.zeros((2 * pair, CHUNK), jnp.float32)
            for ee in range(4):
                both = jnp.concatenate([cbuf[ee, 0, rows(h), :], cbuf[ee, 1, rows(h), :]], axis=0)
                acc += lax.dot_general(
                    both, tbuf[slots, ee * depth : (ee + 1) * depth], NT, preferred_element_type=jnp.float32
                )
            sbuf[h, :, slots] = acc
            sends[h, :, slots] = acc.astype(sends.dtype)

        for d in range(1, layers):
            dev = zpeers[d - 1]
            start(base + d, sends.at[h, pl.ds(pl.multiple_of(dev[2] * half, half), half), :], lands.at[d - 1, h], dev)

    tcopy.wait()
    for k in (6, 7, 10, 13, 15):
        cp[k].wait_recv()
    score(g, 20)

    cp[12].wait_recv()
    start(16, cat(far, yo, o), cat(far, yo, o), mate)
    cp[14].wait_recv()
    start(17, cat(far, y, o), cat(far, y, o), mate)
    for k in (11, 16, 17):
        cp[k].wait_recv()
    score(o, 20 + layers)

    for d in range(1, layers):
        cp[20 + d].wait_recv()
        cp[20 + layers + d].wait_recv()
    for h in range(2):
        total = sbuf[h, pl.ds(pl.multiple_of(l * half, half), half), :]
        for d in range(1, layers):
            total += lands[d - 1, h].astype(jnp.float32)
        o_ref[h * half : (h + 1) * half, :] = total
    for k in cp:
        cp[k].wait_send()


def per_device_fused(layers, query_grads, train_grads, panels, counts):
    _, block, width = query_grads.shape
    train_rows, panel_rows = train_grads[0], panels[0]
    slots, depth, half = train_rows.shape[0], panel_rows.shape[0], block // 2
    bf16 = jnp.bfloat16
    copies = 20 + 2 * layers
    summed = pl.pallas_call(
        functools.partial(kernel, layers),
        out_shape=jax.ShapeDtypeStruct((block, slots), jnp.float32),
        in_specs=[pl.BlockSpec(memory_space=pl.ANY)] * 3,
        out_specs=pl.BlockSpec(memory_space=pltpu.VMEM),
        scratch_shapes=[
            pltpu.VMEM((2, 4 * half, width), bf16),
            pltpu.VMEM((depth, width), bf16),
            pltpu.VMEM((slots, width), bf16),
            pltpu.VMEM((4, 2, 4 * half, depth), bf16),
            pltpu.VMEM((2, 4 * half, slots), jnp.float32),
            pltpu.VMEM((2, 4 * half, slots), bf16),
            pltpu.VMEM((layers - 1, 2, half, slots), bf16),
            pltpu.SemaphoreType.DMA((3,)),
            pltpu.SemaphoreType.DMA((depth // CHUNK,)),
            pltpu.SemaphoreType.DMA((copies,)),
            pltpu.SemaphoreType.DMA((copies,)),
        ],
        compiler_params=pltpu.CompilerParams(
            collective_id=0, has_side_effects=True, vmem_limit_bytes=48 * 2**20
        ),
        cost_estimate=pl.CostEstimate(
            flops=2 * 4 * block * width * (depth + slots), bytes_accessed=2 * width * (block + depth + slots),
            transcendentals=0,
        ),
    )(query_grads.reshape(2, half, width), train_rows, panel_rows)
    alive_mask = (lax.iota(jnp.int32, slots) < counts[0]).astype(jnp.float32)
    factor = 1.0 / math.sqrt(layers * width)
    return summed * (alive_mask * factor)[None, :]


def solution(mesh):
    in_specs = (
        P("layer", "ex", None),
        P("layer", ("groups", "ex"), None),
        P("layer", "ex", None),
        P(("groups", "ex")),
    )
    out_specs = P("layer", ("groups", "ex"))
    shape = dict(mesh.shape)
    body = per_device
    if shape == {"groups": 2, "ex": 4, "layer": 4}:
        body = functools.partial(per_device_fused, shape["layer"])
    return jax.shard_map(body, mesh=mesh, in_specs=in_specs, out_specs=out_specs, check_vma=False)
```

```python
import functools
import math

import jax
import jax.numpy as jnp
from jax import lax
from jax.experimental import pallas as pl
from jax.experimental.pallas import tpu as pltpu
from jax.sharding import PartitionSpec as P

MESH = pl.DeviceIdType.MESH
NT = (((1,), (1,)), ((), ()))
CHUNK = 512
SLOTS = 256


def per_device(query_grads, train_grads, panels, counts):
    train_rows = train_grads[0]
    panel_rows = panels[0]
    column_part = lax.dot_general(
        lax.all_gather(query_grads, "ex", axis=1, tiled=True)[0],
        panel_rows,
        NT,
        preferred_element_type=jnp.float32,
    ).astype(jnp.bfloat16)
    partial_scores = lax.dot_general(
        lax.all_gather(column_part, "ex", axis=1, tiled=True),
        train_rows,
        NT,
        preferred_element_type=jnp.float32,
    )
    alive_mask = (lax.iota(jnp.int32, train_rows.shape[0]) < counts[0]).astype(jnp.float32)
    partial_scores = partial_scores * alive_mask[None, :]
    summed = lax.psum_scatter(partial_scores, "layer", scatter_dimension=0, tiled=True)
    factor = 1.0 / math.sqrt(lax.axis_size("layer") * panel_rows.shape[1])
    return summed * factor


def kernel(layers, q_ref, t_ref, p_ref, o_ref, qbuf, pbuf, tbuf, cbuf, sbuf, sends, lands, loc, psem, send, recv):
    g, e, l = lax.axis_index("groups"), lax.axis_index("ex"), lax.axis_index("layer")
    y, c = e // 2, e % 2
    o = 1 - g
    yo, co = 1 - y, 1 - c
    far = 2 * yo + c
    mate, ypart, xpart = (g, 2 * y + co, l), (g, far, l), (o, e, l)
    half = q_ref.shape[1]
    pair, quarter = 2 * half, half // 2
    depth = p_ref.shape[0]

    def remote(k, src, dst, dev):
        return pltpu.make_async_remote_copy(
            src_ref=src, dst_ref=dst, send_sem=send.at[k], recv_sem=recv.at[k], device_id=dev, device_id_type=MESH
        )

    def qat(yy, hh, cc):
        return qbuf.at[yy, pl.ds(pl.multiple_of(hh * pair + cc * half, half), half), :]

    def rows(hh):
        return pl.ds(pl.multiple_of(hh * pair, pair), pair)

    def cat(ee, yy, hh):
        return cbuf.at[ee, yy, rows(hh), :]

    def piece(ref, s):
        return ref.at[pl.ds(s * quarter, quarter), :]

    def part(ref, s):
        return ref.at[:, pl.ds(s * CHUNK, CHUNK)]

    parts = range(depth // CHUNK)
    own = [pltpu.make_async_copy(q_ref.at[h], qat(y, h, c), loc.at[h]) for h in range(2)]
    pcopy = [
        pltpu.make_async_copy(p_ref.at[pl.ds(j * CHUNK, CHUNK), :], pbuf.at[pl.ds(j * CHUNK, CHUNK), :], psem.at[j])
        for j in parts
    ]
    tcopy = pltpu.make_async_copy(t_ref, tbuf, loc.at[2])
    for d in own + pcopy:
        d.start()

    barrier = pltpu.get_barrier_semaphore()
    zpeers = [(g, e, lax.rem(l + d, layers)) for d in range(1, layers)]
    for dev in zpeers + [ypart, xpart, mate]:
        pl.semaphore_signal(barrier, inc=1, device_id=dev, device_id_type=MESH)
    pl.semaphore_wait(barrier, 2 + layers)

    cp = {}

    def start(name, src, dst, dev):
        k = len(cp)
        cp[name] = remote(k, src, dst, dev)
        cp[name].start()

    def arrived(*names):
        for name in names:
            cp[name].wait_recv()

    for s in range(2):
        start(("qy", s), piece(q_ref.at[g], s), piece(qat(y, g, c), s), ypart)
    for h in range(2):
        start(("qm", h), q_ref.at[h], qat(y, h, c), mate)
    tcopy.start()

    def condition(j, q, yy, where):
        cols = pl.ds(j * CHUNK, CHUNK)
        v = lax.dot_general(q, pbuf[cols, :], NT, preferred_element_type=jnp.float32)
        cbuf[e, yy, where, cols] = v.astype(jnp.bfloat16)

    def hand_on_queries(s):
        arrived(("qy", s))
        got = piece(qat(yo, g, c), s)
        start(("qym", s), got, got, mate)
        start(("qyx", s), got, got, xpart)

    for d in own:
        d.wait()
    arrived(("qm", 0), ("qm", 1))
    for j in parts:
        pcopy[j].wait()
        condition(j, qbuf[y], y, slice(None))
        if j == 0:
            hand_on_queries(0)
    start("ay", cat(e, y, g), cat(e, y, g), ypart)
    hand_on_queries(1)
    for h in range(2):
        start(("am", h), cat(e, y, h), cat(e, y, h), mate)

    arrived(("qym", 0), ("qym", 1))
    for j in parts:
        condition(j, qbuf[yo, rows(g), :], yo, rows(g))
        start(("by", j), part(cat(e, yo, g), j), part(cat(e, yo, g), j), ypart)
        start(("bm", j), part(cat(e, yo, g), j), part(cat(e, yo, g), j), mate)
        if j == 0:
            arrived("ay")
            start("ayx", cat(far, yo, g), cat(far, yo, g), xpart)
            start("aym", cat(far, yo, g), cat(far, yo, g), mate)

    for s in range(2):
        arrived(("qyx", s))
        start(("qxm", s), piece(qat(yo, o, c), s), piece(qat(yo, o, c), s), mate)
    arrived(("qxm", 0), ("qxm", 1))
    for j in parts:
        condition(j, qbuf[yo, rows(o), :], yo, rows(o))
        start(("cm", j), part(cat(e, yo, o), j), part(cat(e, yo, o), j), mate)
        if j == 0:
            for i in parts:
                arrived(("by", i))
                got = part(cat(far, y, g), i)
                start(("byx", i), got, got, xpart)
                start(("bym", i), got, got, mate)

    arrived("ayx")
    start("axm", cat(far, yo, o), cat(far, yo, o), mate)

    def score(h, owners, first, last):
        @pl.loop(0, t_ref.shape[0] // SLOTS)
        def _(j):
            slots = pl.ds(pl.multiple_of(j * SLOTS, SLOTS), SLOTS)
            acc = None if first else sbuf[h, :, slots]
            for ee in owners:
                both = jnp.concatenate([cbuf[ee, 0, rows(h), :], cbuf[ee, 1, rows(h), :]], axis=0)
                span = pl.ds(pl.multiple_of(ee * depth, depth), depth)
                term = lax.dot_general(both, tbuf[slots, span], NT, preferred_element_type=jnp.float32)
                acc = term if acc is None else acc + term
            sbuf[h, :, slots] = acc
            if last:
                sends[h, :, slots] = acc.astype(sends.dtype)

        if last:
            for d in range(1, layers):
                dev = zpeers[d - 1]
                mine = pl.ds(pl.multiple_of(dev[2] * half, half), half)
                start(("z", first, d), sends.at[h, mine, :], lands.at[d - 1, h], dev)

    near, away = [2 * y, 2 * y + 1], [2 * yo, 2 * yo + 1]
    tcopy.wait()
    arrived(("am", 0), ("am", 1), "aym")
    for i in parts:
        arrived(("bm", i), ("bym", i))
    score(g, near + away, True, True)

    for i in parts:
        if i == len(parts) - 1:
            for j in parts:
                arrived(("cm", j))
            score(o, near, True, False)
        arrived(("byx", i))
        got = part(cat(far, y, o), i)
        start(("bxm", i), got, got, mate)
    arrived("axm")
    for i in parts:
        arrived(("bxm", i))
    score(o, away, False, True)

    for d in range(1, layers):
        arrived(("z", True, d), ("z", False, d))
    for h in range(2):
        total = sbuf[h, pl.ds(pl.multiple_of(l * half, half), half), :]
        for d in range(1, layers):
            total += lands[d - 1, h].astype(jnp.float32)
        o_ref[h * half : (h + 1) * half, :] = total
    for name in cp:
        cp[name].wait_send()


def per_device_fused(layers, query_grads, train_grads, panels, counts):
    _, block, width = query_grads.shape
    train_rows, panel_rows = train_grads[0], panels[0]
    slots, depth, half = train_rows.shape[0], panel_rows.shape[0], block // 2
    bf16 = jnp.bfloat16
    copies = 40 + 2 * layers
    summed = pl.pallas_call(
        functools.partial(kernel, layers),
        out_shape=jax.ShapeDtypeStruct((block, slots), jnp.float32),
        in_specs=[pl.BlockSpec(memory_space=pl.ANY)] * 3,
        out_specs=pl.BlockSpec(memory_space=pltpu.VMEM),
        scratch_shapes=[
            pltpu.VMEM((2, 4 * half, width), bf16),
            pltpu.VMEM((depth, width), bf16),
            pltpu.VMEM((slots, width), bf16),
            pltpu.VMEM((4, 2, 4 * half, depth), bf16),
            pltpu.VMEM((2, 4 * half, slots), jnp.float32),
            pltpu.VMEM((2, 4 * half, slots), bf16),
            pltpu.VMEM((layers - 1, 2, half, slots), bf16),
            pltpu.SemaphoreType.DMA((3,)),
            pltpu.SemaphoreType.DMA((depth // CHUNK,)),
            pltpu.SemaphoreType.DMA((copies,)),
            pltpu.SemaphoreType.DMA((copies,)),
        ],
        compiler_params=pltpu.CompilerParams(
            collective_id=0, has_side_effects=True, vmem_limit_bytes=60 * 2**20
        ),
        cost_estimate=pl.CostEstimate(
            flops=2 * 4 * block * width * (depth + slots), bytes_accessed=2 * width * (block + depth + slots),
            transcendentals=0,
        ),
    )(query_grads.reshape(2, half, width), train_rows, panel_rows)
    alive_mask = (lax.iota(jnp.int32, slots) < counts[0]).astype(jnp.float32)
    factor = 1.0 / math.sqrt(layers * width)
    return summed * (alive_mask * factor)[None, :]


def solution(mesh):
    in_specs = (
        P("layer", "ex", None),
        P("layer", ("groups", "ex"), None),
        P("layer", "ex", None),
        P(("groups", "ex")),
    )
    out_specs = P("layer", ("groups", "ex"))
    shape = dict(mesh.shape)
    body = per_device
    if shape == {"groups": 2, "ex": 4, "layer": 4}:
        body = functools.partial(per_device_fused, shape["layer"])
    return jax.shard_map(body, mesh=mesh, in_specs=in_specs, out_specs=out_specs, check_vma=False)
```

```python
import functools
import math

import jax
import jax.numpy as jnp
from jax import lax
from jax.experimental import pallas as pl
from jax.experimental.pallas import tpu as pltpu
from jax.sharding import PartitionSpec as P

MESH = pl.DeviceIdType.MESH
NT = (((1,), (1,)), ((), ()))
CHUNK = 512
SLOTS = 256


def per_device(query_grads, train_grads, panels, counts):
    train_rows = train_grads[0]
    panel_rows = panels[0]
    column_part = lax.dot_general(
        lax.all_gather(query_grads, "ex", axis=1, tiled=True)[0],
        panel_rows,
        NT,
        preferred_element_type=jnp.float32,
    ).astype(jnp.bfloat16)
    partial_scores = lax.dot_general(
        lax.all_gather(column_part, "ex", axis=1, tiled=True),
        train_rows,
        NT,
        preferred_element_type=jnp.float32,
    )
    alive_mask = (lax.iota(jnp.int32, train_rows.shape[0]) < counts[0]).astype(jnp.float32)
    partial_scores = partial_scores * alive_mask[None, :]
    summed = lax.psum_scatter(partial_scores, "layer", scatter_dimension=0, tiled=True)
    factor = 1.0 / math.sqrt(lax.axis_size("layer") * panel_rows.shape[1])
    return summed * factor


def kernel(layers, q_ref, t_ref, p_ref, o_ref, qbuf, pbuf, tbuf, cbuf, sbuf, sends, lands, loc, psem, send, recv):
    g, e, l = lax.axis_index("groups"), lax.axis_index("ex"), lax.axis_index("layer")
    y, c = e // 2, e % 2
    o = 1 - g
    yo, co = 1 - y, 1 - c
    far = 2 * yo + c
    mate, ypart, xpart = (g, 2 * y + co, l), (g, far, l), (o, e, l)
    half = q_ref.shape[1]
    pair, quarter = 2 * half, half // 2
    depth = p_ref.shape[0]

    def remote(k, src, dst, dev):
        return pltpu.make_async_remote_copy(
            src_ref=src, dst_ref=dst, send_sem=send.at[k], recv_sem=recv.at[k], device_id=dev, device_id_type=MESH
        )

    def qat(yy, hh, cc):
        return qbuf.at[yy, pl.ds(pl.multiple_of(hh * pair + cc * half, half), half), :]

    def rows(hh):
        return pl.ds(pl.multiple_of(hh * pair, pair), pair)

    def cat(ee, yy, hh):
        return cbuf.at[ee, yy, rows(hh), :]

    def piece(ref, s):
        return ref.at[pl.ds(s * quarter, quarter), :]

    def part(ref, s):
        return ref.at[:, pl.ds(s * CHUNK, CHUNK)]

    parts = range(depth // CHUNK)
    own = [pltpu.make_async_copy(q_ref.at[h], qat(y, h, c), loc.at[h]) for h in range(2)]
    pcopy = [
        pltpu.make_async_copy(p_ref.at[pl.ds(j * CHUNK, CHUNK), :], pbuf.at[pl.ds(j * CHUNK, CHUNK), :], psem.at[j])
        for j in parts
    ]
    tcopy = pltpu.make_async_copy(t_ref, tbuf, loc.at[2])
    for d in own + pcopy:
        d.start()

    barrier = pltpu.get_barrier_semaphore()
    zpeers = [(g, e, lax.rem(l + d, layers)) for d in range(1, layers)]
    for dev in zpeers + [ypart, xpart, mate]:
        pl.semaphore_signal(barrier, inc=1, device_id=dev, device_id_type=MESH)
    pl.semaphore_wait(barrier, 2 + layers)

    cp = {}

    def start(name, src, dst, dev):
        k = len(cp)
        cp[name] = remote(k, src, dst, dev)
        cp[name].start()

    def arrived(*names):
        for name in names:
            cp[name].wait_recv()

    for s in range(2):
        start(("qy", s), piece(q_ref.at[g], s), piece(qat(y, g, c), s), ypart)
    for h in range(2):
        start(("qm", h), q_ref.at[h], qat(y, h, c), mate)
    tcopy.start()

    def condition(j, q, yy, where):
        cols = pl.ds(j * CHUNK, CHUNK)
        v = lax.dot_general(q, pbuf[cols, :], NT, preferred_element_type=jnp.float32)
        cbuf[e, yy, where, cols] = v.astype(jnp.bfloat16)

    def hand_on_queries(s):
        arrived(("qy", s))
        got = piece(qat(yo, g, c), s)
        start(("qym", s), got, got, mate)
        start(("qyx", s), got, got, xpart)

    for d in own:
        d.wait()
    arrived(("qm", 0), ("qm", 1))
    for j in parts:
        pcopy[j].wait()
        condition(j, qbuf[y], y, slice(None))
    start("ay", cat(e, y, g), cat(e, y, g), ypart)
    for s in range(2):
        hand_on_queries(s)
    for h in range(2):
        start(("am", h), cat(e, y, h), cat(e, y, h), mate)

    arrived(("qym", 0), ("qym", 1))
    for j in parts:
        condition(j, qbuf[yo, rows(g), :], yo, rows(g))
        start(("by", j), part(cat(e, yo, g), j), part(cat(e, yo, g), j), ypart)
        start(("bm", j), part(cat(e, yo, g), j), part(cat(e, yo, g), j), mate)
        if j == 0:
            arrived("ay")
            start("ayx", cat(far, yo, g), cat(far, yo, g), xpart)
            start("aym", cat(far, yo, g), cat(far, yo, g), mate)

    for s in range(2):
        arrived(("qyx", s))
        start(("qxm", s), piece(qat(yo, o, c), s), piece(qat(yo, o, c), s), mate)
    arrived(("qxm", 0), ("qxm", 1))
    for j in parts:
        condition(j, qbuf[yo, rows(o), :], yo, rows(o))
        start(("cm", j), part(cat(e, yo, o), j), part(cat(e, yo, o), j), mate)
        if j == 0:
            for i in parts:
                arrived(("by", i))
                got = part(cat(far, y, g), i)
                start(("byx", i), got, got, xpart)
                start(("bym", i), got, got, mate)

    arrived("ayx")
    start("axm", cat(far, yo, o), cat(far, yo, o), mate)

    def score(h, owners, first, last):
        @pl.loop(0, t_ref.shape[0] // SLOTS)
        def _(j):
            slots = pl.ds(pl.multiple_of(j * SLOTS, SLOTS), SLOTS)
            acc = None if first else sbuf[h, :, slots]
            for ee in owners:
                both = jnp.concatenate([cbuf[ee, 0, rows(h), :], cbuf[ee, 1, rows(h), :]], axis=0)
                span = pl.ds(pl.multiple_of(ee * depth, depth), depth)
                term = lax.dot_general(both, tbuf[slots, span], NT, preferred_element_type=jnp.float32)
                acc = term if acc is None else acc + term
            sbuf[h, :, slots] = acc
            if last:
                sends[h, :, slots] = acc.astype(sends.dtype)

        if last:
            for d in range(1, layers):
                dev = zpeers[d - 1]
                mine = pl.ds(pl.multiple_of(dev[2] * half, half), half)
                start(("z", first, d), sends.at[h, mine, :], lands.at[d - 1, h], dev)

    near, away = [2 * y, 2 * y + 1], [2 * yo, 2 * yo + 1]
    tcopy.wait()
    arrived(("am", 0), ("am", 1), "aym")
    for i in parts:
        arrived(("bm", i), ("bym", i))
    score(g, near + away, True, True)

    for i in parts:
        if i == len(parts) - 1:
            for j in parts:
                arrived(("cm", j))
            score(o, near, True, False)
        arrived(("byx", i))
        got = part(cat(far, y, o), i)
        start(("bxm", i), got, got, mate)
    arrived("axm")
    for i in parts:
        arrived(("bxm", i))
    score(o, away, False, True)

    for d in range(1, layers):
        arrived(("z", True, d), ("z", False, d))
    for h in range(2):
        total = sbuf[h, pl.ds(pl.multiple_of(l * half, half), half), :]
        for d in range(1, layers):
            total += lands[d - 1, h].astype(jnp.float32)
        o_ref[h * half : (h + 1) * half, :] = total
    for name in cp:
        cp[name].wait_send()


def per_device_fused(layers, query_grads, train_grads, panels, counts):
    _, block, width = query_grads.shape
    train_rows, panel_rows = train_grads[0], panels[0]
    slots, depth, half = train_rows.shape[0], panel_rows.shape[0], block // 2
    bf16 = jnp.bfloat16
    copies = 40 + 2 * layers
    summed = pl.pallas_call(
        functools.partial(kernel, layers),
        out_shape=jax.ShapeDtypeStruct((block, slots), jnp.float32),
        in_specs=[pl.BlockSpec(memory_space=pl.ANY)] * 3,
        out_specs=pl.BlockSpec(memory_space=pltpu.VMEM),
        scratch_shapes=[
            pltpu.VMEM((2, 4 * half, width), bf16),
            pltpu.VMEM((depth, width), bf16),
            pltpu.VMEM((slots, width), bf16),
            pltpu.VMEM((4, 2, 4 * half, depth), bf16),
            pltpu.VMEM((2, 4 * half, slots), jnp.float32),
            pltpu.VMEM((2, 4 * half, slots), bf16),
            pltpu.VMEM((layers - 1, 2, half, slots), bf16),
            pltpu.SemaphoreType.DMA((3,)),
            pltpu.SemaphoreType.DMA((depth // CHUNK,)),
            pltpu.SemaphoreType.DMA((copies,)),
            pltpu.SemaphoreType.DMA((copies,)),
        ],
        compiler_params=pltpu.CompilerParams(
            collective_id=0, has_side_effects=True, vmem_limit_bytes=60 * 2**20
        ),
        cost_estimate=pl.CostEstimate(
            flops=2 * 4 * block * width * (depth + slots), bytes_accessed=2 * width * (block + depth + slots),
            transcendentals=0,
        ),
    )(query_grads.reshape(2, half, width), train_rows, panel_rows)
    alive_mask = (lax.iota(jnp.int32, slots) < counts[0]).astype(jnp.float32)
    factor = 1.0 / math.sqrt(layers * width)
    return summed * (alive_mask * factor)[None, :]


def solution(mesh):
    in_specs = (
        P("layer", "ex", None),
        P("layer", ("groups", "ex"), None),
        P("layer", "ex", None),
        P(("groups", "ex")),
    )
    out_specs = P("layer", ("groups", "ex"))
    shape = dict(mesh.shape)
    body = per_device
    if shape == {"groups": 2, "ex": 4, "layer": 4}:
        body = functools.partial(per_device_fused, shape["layer"])
    return jax.shard_map(body, mesh=mesh, in_specs=in_specs, out_specs=out_specs, check_vma=False)
```

```python
import functools
import math

import jax
import jax.numpy as jnp
from jax import lax
from jax.experimental import pallas as pl
from jax.experimental.pallas import tpu as pltpu
from jax.sharding import PartitionSpec as P

MESH = pl.DeviceIdType.MESH
NT = (((1,), (1,)), ((), ()))
CHUNK = 512
SLOTS = 256


def per_device(query_grads, train_grads, panels, counts):
    train_rows = train_grads[0]
    panel_rows = panels[0]
    column_part = lax.dot_general(
        lax.all_gather(query_grads, "ex", axis=1, tiled=True)[0],
        panel_rows,
        NT,
        preferred_element_type=jnp.float32,
    ).astype(jnp.bfloat16)
    partial_scores = lax.dot_general(
        lax.all_gather(column_part, "ex", axis=1, tiled=True),
        train_rows,
        NT,
        preferred_element_type=jnp.float32,
    )
    alive_mask = (lax.iota(jnp.int32, train_rows.shape[0]) < counts[0]).astype(jnp.float32)
    partial_scores = partial_scores * alive_mask[None, :]
    summed = lax.psum_scatter(partial_scores, "layer", scatter_dimension=0, tiled=True)
    factor = 1.0 / math.sqrt(lax.axis_size("layer") * panel_rows.shape[1])
    return summed * factor


def kernel(layers, q_ref, t_ref, p_ref, o_ref, qbuf, pbuf, tbuf, cbuf, sbuf, sends, lands, loc, psem, send, recv):
    g, e, l = lax.axis_index("groups"), lax.axis_index("ex"), lax.axis_index("layer")
    y, c = e // 2, e % 2
    o = 1 - g
    yo, co = 1 - y, 1 - c
    far = 2 * yo + c
    mate, ypart, xpart = (g, 2 * y + co, l), (g, far, l), (o, e, l)
    half = q_ref.shape[1]
    pair, quarter = 2 * half, half // 2
    depth = p_ref.shape[0]

    def remote(k, src, dst, dev):
        return pltpu.make_async_remote_copy(
            src_ref=src, dst_ref=dst, send_sem=send.at[k], recv_sem=recv.at[k], device_id=dev, device_id_type=MESH
        )

    def qat(yy, hh, cc):
        return qbuf.at[yy, pl.ds(pl.multiple_of(hh * pair + cc * half, half), half), :]

    def rows(hh):
        return pl.ds(pl.multiple_of(hh * pair, pair), pair)

    def cat(ee, yy, hh):
        return cbuf.at[ee, yy, rows(hh), :]

    def piece(ref, s):
        return ref.at[pl.ds(s * quarter, quarter), :]

    def part(ref, s):
        return ref.at[:, pl.ds(s * CHUNK, CHUNK)]

    parts = range(depth // CHUNK)
    own = [pltpu.make_async_copy(q_ref.at[h], qat(y, h, c), loc.at[h]) for h in range(2)]
    pcopy = [
        pltpu.make_async_copy(p_ref.at[pl.ds(j * CHUNK, CHUNK), :], pbuf.at[pl.ds(j * CHUNK, CHUNK), :], psem.at[j])
        for j in parts
    ]
    tcopy = pltpu.make_async_copy(t_ref, tbuf, loc.at[2])
    for d in own + pcopy:
        d.start()

    barrier = pltpu.get_barrier_semaphore()
    zpeers = [(g, e, lax.rem(l + d, layers)) for d in range(1, layers)]
    for dev in zpeers + [ypart, xpart, mate]:
        pl.semaphore_signal(barrier, inc=1, device_id=dev, device_id_type=MESH)
    pl.semaphore_wait(barrier, 2 + layers)

    cp = {}

    def start(name, src, dst, dev):
        k = len(cp)
        cp[name] = remote(k, src, dst, dev)
        cp[name].start()

    def arrived(*names):
        for name in names:
            cp[name].wait_recv()

    for s in range(2):
        start(("qy", s), piece(q_ref.at[g], s), piece(qat(y, g, c), s), ypart)
    for h in range(2):
        start(("qm", h), q_ref.at[h], qat(y, h, c), mate)
    tcopy.start()

    def condition(j, q, yy, where):
        cols = pl.ds(j * CHUNK, CHUNK)
        v = lax.dot_general(pbuf[cols, :], q, NT, preferred_element_type=jnp.float32)
        cbuf[e, yy, where, cols] = v.astype(jnp.bfloat16).T

    def hand_on_queries(s):
        arrived(("qy", s))
        got = piece(qat(yo, g, c), s)
        start(("qym", s), got, got, mate)
        start(("qyx", s), got, got, xpart)

    for d in own:
        d.wait()
    arrived(("qm", 0), ("qm", 1))
    for j in parts:
        pcopy[j].wait()
        condition(j, qbuf[y], y, slice(None))
        if j == 0:
            hand_on_queries(0)
    start("ay", cat(e, y, g), cat(e, y, g), ypart)
    hand_on_queries(1)
    for h in range(2):
        start(("am", h), cat(e, y, h), cat(e, y, h), mate)

    arrived(("qym", 0), ("qym", 1))
    for j in parts:
        condition(j, qbuf[yo, rows(g), :], yo, rows(g))
        start(("by", j), part(cat(e, yo, g), j), part(cat(e, yo, g), j), ypart)
        start(("bm", j), part(cat(e, yo, g), j), part(cat(e, yo, g), j), mate)
        if j == 0:
            arrived("ay")
            start("ayx", cat(far, yo, g), cat(far, yo, g), xpart)
            start("aym", cat(far, yo, g), cat(far, yo, g), mate)

    for s in range(2):
        arrived(("qyx", s))
        start(("qxm", s), piece(qat(yo, o, c), s), piece(qat(yo, o, c), s), mate)
    arrived(("qxm", 0), ("qxm", 1))
    for j in parts:
        condition(j, qbuf[yo, rows(o), :], yo, rows(o))
        start(("cm", j), part(cat(e, yo, o), j), part(cat(e, yo, o), j), mate)
        if j == 0:
            for i in parts:
                arrived(("by", i))
                got = part(cat(far, y, g), i)
                start(("byx", i), got, got, xpart)
                start(("bym", i), got, got, mate)

    arrived("ayx")
    start("axm", cat(far, yo, o), cat(far, yo, o), mate)

    def score(h, owners, first, last):
        @pl.loop(0, t_ref.shape[0] // SLOTS)
        def _(j):
            slots = pl.ds(pl.multiple_of(j * SLOTS, SLOTS), SLOTS)
            acc = None if first else sbuf[h, :, slots]
            for ee in owners:
                both = jnp.concatenate([cbuf[ee, 0, rows(h), :], cbuf[ee, 1, rows(h), :]], axis=0)
                span = pl.ds(pl.multiple_of(ee * depth, depth), depth)
                term = lax.dot_general(both, tbuf[slots, span], NT, preferred_element_type=jnp.float32)
                acc = term if acc is None else acc + term
            sbuf[h, :, slots] = acc
            if last:
                sends[h, :, slots] = acc.astype(sends.dtype)

        if last:
            for d in range(1, layers):
                dev = zpeers[d - 1]
                mine = pl.ds(pl.multiple_of(dev[2] * half, half), half)
                start(("z", first, d), sends.at[h, mine, :], lands.at[d - 1, h], dev)

    near, away = [2 * y, 2 * y + 1], [2 * yo, 2 * yo + 1]
    tcopy.wait()
    arrived(("am", 0), ("am", 1), "aym")
    for i in parts:
        arrived(("bm", i), ("bym", i))
    score(g, near + away, True, True)

    for i in parts:
        if i == len(parts) - 1:
            for j in parts:
                arrived(("cm", j))
            score(o, near, True, False)
        arrived(("byx", i))
        got = part(cat(far, y, o), i)
        start(("bxm", i), got, got, mate)
    arrived("axm")
    for i in parts:
        arrived(("bxm", i))
    score(o, away, False, True)

    for d in range(1, layers):
        arrived(("z", True, d), ("z", False, d))
    for h in range(2):
        total = sbuf[h, pl.ds(pl.multiple_of(l * half, half), half), :]
        for d in range(1, layers):
            total += lands[d - 1, h].astype(jnp.float32)
        o_ref[h * half : (h + 1) * half, :] = total
    for name in cp:
        cp[name].wait_send()


def per_device_fused(layers, query_grads, train_grads, panels, counts):
    _, block, width = query_grads.shape
    train_rows, panel_rows = train_grads[0], panels[0]
    slots, depth, half = train_rows.shape[0], panel_rows.shape[0], block // 2
    bf16 = jnp.bfloat16
    copies = 40 + 2 * layers
    summed = pl.pallas_call(
        functools.partial(kernel, layers),
        out_shape=jax.ShapeDtypeStruct((block, slots), jnp.float32),
        in_specs=[pl.BlockSpec(memory_space=pl.ANY)] * 3,
        out_specs=pl.BlockSpec(memory_space=pltpu.VMEM),
        scratch_shapes=[
            pltpu.VMEM((2, 4 * half, width), bf16),
            pltpu.VMEM((depth, width), bf16),
            pltpu.VMEM((slots, width), bf16),
            pltpu.VMEM((4, 2, 4 * half, depth), bf16),
            pltpu.VMEM((2, 4 * half, slots), jnp.float32),
            pltpu.VMEM((2, 4 * half, slots), bf16),
            pltpu.VMEM((layers - 1, 2, half, slots), bf16),
            pltpu.SemaphoreType.DMA((3,)),
            pltpu.SemaphoreType.DMA((depth // CHUNK,)),
            pltpu.SemaphoreType.DMA((copies,)),
            pltpu.SemaphoreType.DMA((copies,)),
        ],
        compiler_params=pltpu.CompilerParams(
            collective_id=0, has_side_effects=True, vmem_limit_bytes=60 * 2**20
        ),
        cost_estimate=pl.CostEstimate(
            flops=2 * 4 * block * width * (depth + slots), bytes_accessed=2 * width * (block + depth + slots),
            transcendentals=0,
        ),
    )(query_grads.reshape(2, half, width), train_rows, panel_rows)
    alive_mask = (lax.iota(jnp.int32, slots) < counts[0]).astype(jnp.float32)
    factor = 1.0 / math.sqrt(layers * width)
    return summed * (alive_mask * factor)[None, :]


def solution(mesh):
    in_specs = (
        P("layer", "ex", None),
        P("layer", ("groups", "ex"), None),
        P("layer", "ex", None),
        P(("groups", "ex")),
    )
    out_specs = P("layer", ("groups", "ex"))
    shape = dict(mesh.shape)
    body = per_device
    if shape == {"groups": 2, "ex": 4, "layer": 4}:
        body = functools.partial(per_device_fused, shape["layer"])
    return jax.shard_map(body, mesh=mesh, in_specs=in_specs, out_specs=out_specs, check_vma=False)
```
